32 devices in a mesh: group: 8 (over z, y), inner: 4 (over x, core).
Axes of the slice: x: 2, y: 2, z: 4, core: 2. Of those that a mesh axis runs over, the one named last changes fastest.
Arguments:
- tokens: bfloat16 [1024, 7168], P('group', 'inner'), may hold values from -6 to 6
- routes: int32 [1024, 4], P('group'), may hold values from 0 to 7, all different within a row; in each aligned block of 128 rows (0 to 127, 128 to 255, ...) at most 96 rows name the same one
- gate_weights: float32 [1024, 4], P('group'), may hold values from 0.1 to 1
- w_gate: bfloat16 [8, 7168, 2048], P('group', None, 'inner'), may hold values from -0.0625 to 0.0625
- w_up: bfloat16 [8, 7168, 2048], P('group', None, 'inner'), may hold values from -0.0625 to 0.0625
- w_down: bfloat16 [8, 2048, 7168], P('group', 'inner'), may hold values from -0.125 to 0.125
Outputs:
- moe_out: bfloat16 [1024, 7168], P('group', 'inner')
The draws below stay inside these ranges and needn't reach their ends.
Inputs may be any that keep to these rules, and one draw needn't show every extreme that they name: `routes`: each row names 4 different expert groups. Within each aligned block of 128 rows (the rows of one index of group) no group is named by more than 96 rows, and in some blocks one group is named by exactly 96 rows.
All inputs are finite; a program needn't handle non-finite values.
Results may differ from the reference program's by a relative error of at most 0.014.
Values may be sent and summed in bfloat16 or wider, within the bound.
No kernel may reach another device: no remote copies, remote signals or barrier semaphores. Data moves between devices by JAX's collectives and lax.ppermute only.
A program may use at most 128 MiB of HBM per device.

```python
import math
import jax
import jax.numpy as jnp
import numpy as np
from jax import lax

D = 7168
FE = 2048
CHOSEN = 4
TOK_GROUP = 128
CAP = 96
EXPERTS = 8
TOKENS = 1024
N_GROUP = 8
N_INNER = 4


def levels(key, shape, pieces, least, largest):
    gain = 1.0
    for axis_at, blocks in pieces:
        heights = jax.random.uniform(jax.random.fold_in(jax.random.fold_in(key, 6), axis_at), (blocks,), jnp.float32, least / len(pieces), largest / len(pieces))
        gain = gain * jnp.repeat(jnp.exp(heights), shape[axis_at] // blocks).reshape((-1,) + (1,) * (len(shape) - 1 - axis_at))
    return gain


def deal_out(own_key, own, number, rows, count, top, bound, skew):
    ranking = jax.random.permutation(own_key, count)
    crowded, common = shares(count, rows * top, bound, skew, True), shares(count, rows * top, bound, skew, False)
    places = jnp.arange(count)

    def named(tallies, rotation):
        used = int((tallies > 0).sum())
        fixed = max(1, used // 4)
        passed = fixed + (places - fixed + rotation * (used - fixed)) % max(1, count - fixed)
        return jnp.zeros((count,), jnp.int32).at[ranking[jnp.where(places < fixed, places, passed)]].set(jnp.asarray(tallies, jnp.int32))

    tallies = jnp.where(number % 4 == 0, named(crowded, number // 4), named(common, number - number // 4 - 1))
    mixed = jax.random.permutation(jax.random.fold_in(own, 3), count)
    donor, receiver = mixed[0:count // 2 * 2:2], mixed[1:count // 2 * 2:2]
    margin = jnp.minimum(tallies[donor] - 1, bound - tallies[receiver]) // 2
    margin = jnp.where((donor == ranking[0]) | (receiver == ranking[0]) | (tallies[receiver] == 0), 0, jnp.maximum(margin, 0))
    passed = jax.random.randint(jax.random.fold_in(own, 4), (count // 2,), 0, 1 << 20) % (margin + 1)
    tallies = tallies.at[donor].add(-passed).at[receiver].add(passed)
    members = jnp.searchsorted(jnp.cumsum(tallies), jnp.arange(rows * top), side="right").astype(jnp.int32)
    table = members.reshape(top, rows).T
    table = table[jax.random.permutation(jax.random.fold_in(own, 1), rows)]
    rotation = jax.random.randint(jax.random.fold_in(own, 2), (rows, 1), 0, top)
    return jnp.take_along_axis(table, (jnp.arange(top)[None, :] + rotation) % top, axis=1)


def shares(number_of, total, most, lean, full):
    weights = [(1 << 20) // math.isqrt(standing ** lean) + 1 for standing in range(1, number_of + 1)]
    largest = most if full else min(most, max(-(-total // number_of), total * weights[0] // sum(weights)))
    least = 1 if total - largest >= number_of - 1 else 0
    given, rest = [largest] + [least] * (number_of - 1), total - largest - least * (number_of - 1)
    while rest > 0:
        movable = [i for i in range(1, number_of) if given[i] < largest] or [i for i in range(1, number_of) if given[i] < most]
        whole, budget = sum([weights[i] for i in movable]), rest
        for i in movable:
            addition = min(most - given[i], max(1, budget * weights[i] // whole), rest)
            given[i] = given[i] + addition
            rest = rest - addition
    return np.array(given)


def normal_values(key, dims, width, reach, pieces=(), held_as=jnp.bfloat16):
    gain = levels(key, dims, pieces, -0.22, 0.18) if pieces else 1.0
    drawn = jax.random.normal(key, dims, jnp.float32) * width * gain
    return jnp.minimum(jnp.maximum(drawn, -reach), reach).astype(held_as)


def setup_inputs(seed: int = 0) -> dict:
    keys = jax.random.split(jax.random.key(seed), 7)
    tokens = normal_values(keys[0], (TOKENS, D), 1.0, 6.0, ((0, 8), (1, 4)))
    routes_keys = jax.random.split(jax.random.fold_in(keys[1], 1), TOKENS // TOK_GROUP)
    routes_turns = jax.random.permutation(jax.random.fold_in(keys[1], 3), TOKENS // TOK_GROUP)
    routes = jax.vmap(lambda own, number: deal_out(jax.random.fold_in(keys[1], 2), own, number, TOK_GROUP, N_GROUP, CHOSEN, CAP, 2))(routes_keys, routes_turns).reshape((TOKENS, CHOSEN))
    gate_weights = jnp.clip(0.1 + 0.9 * jax.random.uniform(keys[2], (TOKENS, CHOSEN), jnp.float32) ** levels(keys[2], (TOKENS, CHOSEN), ((0, 8),), -0.2, 0.2), 0.1, 1.0)
    w_gate = normal_values(keys[3], (EXPERTS, D, FE), D ** -0.5, 0.0625, ((0, 8), (2, 4)))
    w_up = normal_values(keys[4], (EXPERTS, D, FE), D ** -0.5, 0.0625, ((0, 8), (2, 4)))
    w_down = normal_values(keys[5], (EXPERTS, FE, D), FE ** -0.5, 0.125, ((0, 8), (1, 4)))
    return dict(tokens=tokens, routes=routes, gate_weights=gate_weights, w_gate=w_gate, w_up=w_up, w_down=w_down)


def expert_rows(token_rows, gate_mat, up_mat, down_mat, parts):
    gate_out = jnp.dot(token_rows, gate_mat, preferred_element_type=jnp.float32)
    up_out = jnp.dot(token_rows, up_mat, preferred_element_type=jnp.float32)
    hidden = (jax.nn.silu(gate_out) * up_out).astype(jnp.bfloat16)
    span_size = hidden.shape[1] // parts
    summed = jnp.zeros((token_rows.shape[0], down_mat.shape[1]), jnp.float32)
    for slice_id in range(parts):
        lower = slice_id * span_size
        partial_value = jnp.dot(hidden[:, lower:lower + span_size], down_mat[lower:lower + span_size], preferred_element_type=jnp.float32)
        rounded = lax.optimization_barrier(partial_value.astype(jnp.bfloat16))
        summed = summed + rounded.astype(jnp.float32)
    return summed


def reference(tokens, routes, gate_weights, w_gate, w_up, w_down):
    route_blocks = routes.reshape(N_GROUP, TOK_GROUP, CHOSEN)
    group_ids = jnp.arange(N_GROUP, dtype=jnp.int32)
    onehot = route_blocks[..., None] == group_ids
    chosen = jnp.sum(onehot.astype(jnp.int32), axis=2)
    weight_by = jnp.sum(jnp.where(onehot, gate_weights.reshape(N_GROUP, TOK_GROUP, CHOSEN)[..., None], 0.0), axis=2).astype(jnp.float32)
    slot_of = jnp.cumsum(chosen, axis=1) - 1
    token_blocks = tokens.reshape(N_GROUP, TOK_GROUP, D).astype(jnp.float32)
    slot_ids = jnp.arange(CAP, dtype=jnp.int32)

    def one_expert(totals, expert_id):
        picked = lax.dynamic_index_in_dim(chosen, expert_id, 2, keepdims=False)
        position = lax.dynamic_index_in_dim(slot_of, expert_id, 2, keepdims=False)
        weight_one = lax.dynamic_index_in_dim(weight_by, expert_id, 2, keepdims=False)
        placing = ((picked[:, None, :] == 1) & (position[:, None, :] == slot_ids[None, :, None])).astype(jnp.float32)
        gathered = jnp.einsum("sct,std->scd", placing, token_blocks, precision=lax.Precision.HIGHEST)
        gathered = gathered.astype(jnp.bfloat16).reshape(N_GROUP * CAP, D)
        out_rows = expert_rows(gathered, w_gate[expert_id], w_up[expert_id], w_down[expert_id], N_INNER)
        out_blocks = out_rows.reshape(N_GROUP, CAP, D)
        weight_table = placing * weight_one[:, None, :]
        totals = totals + jnp.einsum("sct,scd->std", weight_table, out_blocks, precision=lax.Precision.HIGHEST)
        return totals, expert_id

    summed, unused_ids = lax.scan(one_expert, jnp.zeros((N_GROUP, TOK_GROUP, D), jnp.float32), jnp.arange(N_GROUP, dtype=jnp.int32))
    return summed.reshape(TOKENS, D).astype(jnp.bfloat16)
```

```python
import jax
import jax.numpy as jnp
from jax import lax
from jax.sharding import PartitionSpec as P

BF = jnp.bfloat16
F32 = jnp.float32


def routing(routes, gate_weights, groups):
    onehot = routes[:, :, None] == jnp.arange(groups, dtype=jnp.int32)
    weight = jnp.sum(jnp.where(onehot, gate_weights[:, :, None], 0.0), axis=1).T
    picked = jnp.any(onehot, axis=1).T
    rows = routes.shape[0]
    before = jnp.arange(rows)[:, None] < jnp.arange(rows)[None, :]
    slot = jnp.dot(picked.astype(BF), before.astype(BF), preferred_element_type=F32)
    return jnp.stack([jnp.where(picked, slot, -1.0), weight])


def local(tokens, routes, gate_weights, w_gate, w_up, w_down):
    groups, inners = lax.axis_size("group"), lax.axis_size("inner")
    g, i = lax.axis_index("group"), lax.axis_index("inner")
    chips, planes = inners // 2, groups // 2
    x, c = i // 2, i % 2
    rows, feats = tokens.shape
    cap = rows * routes.shape[1] * 3 // (2 * groups)
    depth = w_down.shape[2]

    def over_y(a):
        return lax.ppermute(a, "group", [(j, j ^ 1) for j in range(groups)])

    def over_z(a):
        return lax.ppermute(a, "group", [(j, (j + 2) % groups) for j in range(groups)])

    def over_core(a):
        return lax.ppermute(a, "inner", [(j, j ^ 1) for j in range(inners)])

    def over_x(a, s):
        return lax.ppermute(a, "inner", [(j, (j + 2 * s) % inners) for j in range(inners)])

    info = routing(routes, gate_weights, groups)
    infos = [jnp.stack([info, over_y(info)])]
    main = [tokens]
    for t in range(1, planes):
        infos.append(over_z(infos[-1]))
        main.append(over_z(main[-1]))
    other = [over_y(a) for a in main]

    slots = jnp.arange(cap, dtype=jnp.int32).astype(F32)
    q = []
    for t in range(planes):
        mine = lax.dynamic_index_in_dim(infos[t], g, 2, keepdims=False)
        packed, parts = [], [[] for _ in range(chips)]
        for u, block in enumerate((main[t], other[t])):
            placing = (mine[u, 0][None, :] == slots[:, None]).astype(BF)
            p = jnp.dot(placing, block, preferred_element_type=F32).astype(BF)
            for s in range(chips):
                parts[s].append(p if s == 0 else over_x(p, s))
        parts = [jnp.concatenate(p, axis=0) for p in parts]
        ordered = []
        for k in range(chips):
            value = parts[0]
            for s in range(1, chips):
                value = jnp.where((x - s) % chips == k, parts[s], value)
            ordered.append(value)
        half = jnp.stack(ordered, axis=1)
        far = over_core(half)
        even, odd = jnp.where(c == 0, half, far), jnp.where(c == 0, far, half)
        full = jnp.stack([even, odd], axis=2).reshape(2 * cap, depth)
        gate = jnp.dot(full, w_gate[0], preferred_element_type=F32)
        up = jnp.dot(full, w_up[0], preferred_element_type=F32)
        hidden = (jax.nn.silu(gate) * up).astype(BF)
        part = jnp.dot(hidden, w_down[0], preferred_element_type=F32).astype(BF)
        part = part.reshape(2 * cap, chips, 2, feats)
        keep = jnp.where(c == 0, part[:, :, 0], part[:, :, 1])
        give = jnp.where(c == 0, part[:, :, 1], part[:, :, 0])
        pair = keep.astype(F32) + over_core(give).astype(F32)
        weighted = []
        for u in (0, 1):
            here = pair[u * cap:(u + 1) * cap]
            total = lax.dynamic_index_in_dim(here, x, 1, keepdims=False)
            for s in range(1, chips):
                away = lax.dynamic_index_in_dim(here, (x + s) % chips, 1, keepdims=False)
                total = total + over_x(away.astype(BF), s).astype(F32)
            back = (mine[u, 0][:, None] == slots[None, :]).astype(BF)
            spread = jnp.dot(back, total.astype(BF), preferred_element_type=F32)
            weighted.append(spread * mine[u, 1][:, None])
        q.append(weighted[0] + over_y(weighted[1].astype(BF)).astype(F32))

    total = q[1 % planes]
    for t in range(2, planes + 1):
        total = over_z(total.astype(BF)).astype(F32) + q[t % planes]
    return total.astype(BF)


def solution(mesh):
    placed = (
        P("group", "inner"),
        P("group", None),
        P("group", None),
        P("group", None, "inner"),
        P("group", None, "inner"),
        P("group", "inner", None),
    )
    return jax.shard_map(
        local, mesh=mesh, in_specs=placed, out_specs=P("group", "inner"), check_vma=False
    )
```

```python
import functools

import jax
import jax.numpy as jnp
from jax import lax
from jax.experimental import pallas as pl
from jax.experimental.pallas import tpu as pltpu
from jax.sharding import PartitionSpec as P

BF = jnp.bfloat16
F32 = jnp.float32


def routing(routes, gate_weights, groups):
    onehot = routes[:, :, None] == jnp.arange(groups, dtype=jnp.int32)
    weight = jnp.sum(jnp.where(onehot, gate_weights[:, :, None], 0.0), axis=1).T
    picked = jnp.any(onehot, axis=1).T
    rows = routes.shape[0]
    before = jnp.arange(rows)[:, None] < jnp.arange(rows)[None, :]
    slot = jnp.dot(picked.astype(BF), before.astype(BF), preferred_element_type=F32)
    return jnp.stack([jnp.where(picked, slot, -1.0), weight])


def expert_kernel(pieces, order, near, far, w_gate, w_up, w_down, give, keep, gate, up, hidden):
    k = pl.program_id(0)
    both = 2 * pieces

    def add(rows):
        gate_part = jnp.dot(rows[...], w_gate[...], preferred_element_type=F32)
        up_part = jnp.dot(rows[...], w_up[...], preferred_element_type=F32)
        gate[...] += gate_part
        up[...] += up_part

    @pl.when(k == 0)
    def _():
        gate[...] = jnp.zeros_like(gate)
        up[...] = jnp.zeros_like(up)

    @pl.when(k < pieces)
    def _():
        add(near)

    @pl.when((k >= pieces) & (k < both))
    def _():
        add(far)

    @pl.when(k == both - 1)
    def _():
        v = gate[...]
        hidden[...] = (v / (1.0 + jnp.exp(-v)) * up[...]).astype(BF)

    @pl.when((k >= both) & (k < both + pieces))
    def _():
        give[...] = jnp.dot(hidden[...], w_down[...], preferred_element_type=F32).astype(BF)

    @pl.when(k >= both + pieces)
    def _():
        keep[...] = jnp.dot(hidden[...], w_down[...], preferred_element_type=F32).astype(BF)


def expert(order, near, far, w_gate, w_up, w_down, feats):
    rows, width = near.shape
    pieces = width // feats
    both = 2 * pieces
    units = w_down.shape[1]

    def at(low, high):
        return lambda k, order: (0, jnp.clip(k - low, 0, high - low - 1))

    grid = pltpu.PrefetchScalarGridSpec(
        num_scalar_prefetch=1,
        grid=(2 * both,),
        in_specs=[
            pl.BlockSpec((rows, feats), at(0, pieces)),
            pl.BlockSpec((rows, feats), at(pieces, both)),
            pl.BlockSpec((None, feats, units), lambda k, order: (0, order[jnp.minimum(k, both - 1)], 0)),
            pl.BlockSpec((None, feats, units), lambda k, order: (0, order[jnp.minimum(k, both - 1)], 0)),
            pl.BlockSpec((None, units, feats), lambda k, order: (0, 0, order[jnp.maximum(k, both)])),
        ],
        out_specs=[
            pl.BlockSpec((rows, feats), at(both, both + pieces)),
            pl.BlockSpec((rows, feats), at(both + pieces, 2 * both)),
        ],
        scratch_shapes=[
            pltpu.VMEM((rows, units), F32),
            pltpu.VMEM((rows, units), F32),
            pltpu.VMEM((rows, units), BF),
        ],
    )
    depth = w_gate.shape[1]
    return pl.pallas_call(
        functools.partial(expert_kernel, pieces),
        grid_spec=grid,
        out_shape=[jax.ShapeDtypeStruct((rows, width), BF)] * 2,
        compiler_params=pltpu.CompilerParams(vmem_limit_bytes=28 * 2**20),
        cost_estimate=pl.CostEstimate(
            flops=6 * rows * depth * units,
            bytes_accessed=6 * depth * units + 8 * rows * width,
            transcendentals=rows * units,
        ),
    )(order, near, far, w_gate, w_up, w_down)


def local(tokens, routes, gate_weights, w_gate, w_up, w_down):
    groups, inners = lax.axis_size("group"), lax.axis_size("inner")
    g, i = lax.axis_index("group"), lax.axis_index("inner")
    chips, planes = inners // 2, groups // 2
    x, c = i // 2, i % 2
    rows, feats = tokens.shape
    cap = rows * routes.shape[1] * 3 // (2 * groups)

    def over_y(a):
        return lax.ppermute(a, "group", [(j, j ^ 1) for j in range(groups)])

    def over_z(a):
        return lax.ppermute(a, "group", [(j, (j + 2) % groups) for j in range(groups)])

    def over_core(a):
        return lax.ppermute(a, "inner", [(j, j ^ 1) for j in range(inners)])

    def over_x(a, s):
        return lax.ppermute(a, "inner", [(j, (j + 2 * s) % inners) for j in range(inners)])

    came = [(x - s) % chips * 2 for s in range(chips)]
    goes = [(x + s) % chips * 2 for s in range(chips)]
    order = jnp.stack(
        [k + c for k in came] + [k + 1 - c for k in came] + [k + 1 - c for k in goes] + [k + c for k in goes]
    ).astype(jnp.int32)

    info = routing(routes, gate_weights, groups)
    infos = [jnp.stack([info, over_y(info)])]
    main = [tokens]
    for t in range(1, planes):
        infos.append(over_z(infos[-1]))
        main.append(over_z(main[-1]))
    other = [over_y(a) for a in main]

    slots = jnp.arange(cap, dtype=jnp.int32).astype(F32)
    q = []
    for t in range(planes):
        mine = lax.dynamic_index_in_dim(infos[t], g, 2, keepdims=False)
        blocks = []
        for u, block in enumerate((main[t], other[t])):
            placing = (mine[u, 0][None, :] == slots[:, None]).astype(BF)
            p = jnp.dot(placing, block, preferred_element_type=F32).astype(BF)
            blocks.append([p] + [over_x(p, s) for s in range(1, chips)])
        near = jnp.block(blocks)
        give, keep = expert(order, near, over_core(near), w_gate, w_up, w_down, feats)
        pair = keep.astype(F32) + over_core(give).astype(F32)
        weighted = []
        for u in (0, 1):
            here = pair[u * cap:(u + 1) * cap]
            total = here[:, :feats]
            for s in range(1, chips):
                total = total + over_x(here[:, s * feats:(s + 1) * feats].astype(BF), s).astype(F32)
            back = (mine[u, 0][:, None] == slots[None, :]).astype(BF)
            spread = jnp.dot(back, total.astype(BF), preferred_element_type=F32)
            weighted.append(spread * mine[u, 1][:, None])
        q.append(weighted[0] + over_y(weighted[1].astype(BF)).astype(F32))

    total = q[1 % planes]
    for t in range(2, planes + 1):
        total = over_z(total.astype(BF)).astype(F32) + q[t % planes]
    return total.astype(BF)


def solution(mesh):
    placed = (
        P("group", "inner"),
        P("group", None),
        P("group", None),
        P("group", None, "inner"),
        P("group", None, "inner"),
        P("group", "inner", None),
    )
    return jax.shard_map(
        local, mesh=mesh, in_specs=placed, out_specs=P("group", "inner"), check_vma=False
    )
```

```python
import functools

import jax
import jax.numpy as jnp
from jax import lax
from jax.experimental import pallas as pl
from jax.experimental.pallas import tpu as pltpu
from jax.sharding import PartitionSpec as P

BF = jnp.bfloat16
F32 = jnp.float32
TOKEN = jax.ShapeDtypeStruct((8, 128), F32)
PACK, EXPERT, PAIR, SPREAD, LABEL = 10, 40, 0.7, 1.5, 1.0
VMEM_MIB, EXPERT_MIB = 12, 22


def behind(kernel, reads, after):
    return lambda *refs: kernel(*refs[:reads], *refs[reads + after:])


def call(kernel, out_shape, specs, operands, after, us, mib=VMEM_MIB):
    vmem = pl.BlockSpec(memory_space=pltpu.VMEM)
    return pl.pallas_call(
        behind(kernel, len(operands), len(after)),
        in_specs=[s or vmem for s in specs] + [pl.BlockSpec(memory_space=pl.ANY)] * len(after),
        out_specs=[vmem] * (len(out_shape) + 1),
        out_shape=[*out_shape, TOKEN],
        compiler_params=pltpu.CompilerParams(vmem_limit_bytes=mib * 2**20),
        cost_estimate=hint(us),
    )(*operands, *after)


def hint(us):
    return pl.CostEstimate(flops=int(us * 1e9), bytes_accessed=1024, transcendentals=0)


SMEM = pl.BlockSpec(memory_space=pltpu.SMEM)


def label_kernel(tokens, routes, weights, block, token):
    rows = tokens.shape[0]
    block[:rows, :] = tokens[...]
    w = weights[...]
    high = w.astype(BF).astype(F32)
    middle = (w - high).astype(BF).astype(F32)
    low = w - high - middle
    spare = block.shape[0] - rows - 4 * w.shape[0]
    parts = [routes[...].astype(F32), high, middle, low] + [jnp.zeros((spare, rows), F32)] * (spare > 0)
    block[rows:, :rows] = jnp.concatenate(parts, axis=0).astype(BF)
    if block.shape[1] > rows:
        block[rows:, rows:] = jnp.zeros((block.shape[0] - rows, block.shape[1] - rows), BF)
    token[...] = jnp.zeros_like(token)


def label(tokens, routes, gate_weights, after):
    rows, feats = tokens.shape
    extra = -(-4 * routes.shape[1] // 16) * 16
    out = [jax.ShapeDtypeStruct((rows + extra, feats), BF)]
    return call(label_kernel, out, [None] * 3, (tokens, routes.T, gate_weights.T), after, LABEL)


def placing_of(labels, me, cap, choices):
    rows = labels.shape[1]
    named = labels[:choices] == me.astype(F32)
    weights = labels[choices:2 * choices] + labels[2 * choices:3 * choices] + labels[3 * choices:4 * choices]
    weight = jnp.sum(jnp.where(named, weights, 0.0), axis=0, keepdims=True)
    picked = jnp.sum(jnp.where(named, 1.0, 0.0), axis=0, keepdims=True)
    one, two = (lax.broadcasted_iota(jnp.int32, (rows, rows), n) for n in (0, 1))
    before = jnp.where(one < two, 1.0, 0.0).astype(BF)
    many = jnp.broadcast_to(picked, (16, rows)).astype(BF)
    slot = jnp.dot(many, before, preferred_element_type=F32)[:1]
    slot = jnp.where(picked > 0.5, slot, -1.0).astype(jnp.int32)
    return lax.broadcasted_iota(jnp.int32, (cap, rows), 0) == slot, weight


def joined(pieces, near):
    feats = pieces[0].shape[1]
    for n, piece in enumerate(pieces):
        near[:, n * feats:(n + 1) * feats] = piece[...]


def join_kernel(*refs):
    *pieces, near, token = refs
    joined(pieces, near)
    token[...] = jnp.zeros_like(token)


def side_by_side(pieces):
    return [jax.ShapeDtypeStruct((pieces[0].shape[0], len(pieces) * pieces[0].shape[1]), BF)] if pieces else []


def join(pieces, after):
    return call(join_kernel, side_by_side(pieces), [None] * len(pieces), pieces, after, PACK)


def pack_kernel(choices, ahead, before, at, *refs):
    blocks, following, pieces = refs[:2], refs[2:2 + ahead], refs[2 + ahead:2 + ahead + before]
    packed, labels, *rest, token = refs[2 + ahead + before:]
    for a, b in zip(following, rest[:ahead], strict=True):
        b[...] = a[...]
    if before:
        joined(pieces, rest[ahead])
    rows, cap = labels.shape[2], packed.shape[0] // len(blocks)
    parts = []
    for u, block in enumerate(blocks):
        lines = block[rows:, :rows].astype(F32)
        labels[u] = lines
        placing, _ = placing_of(lines, at[0], cap, choices)
        placing = jnp.where(placing, 1.0, 0.0).astype(BF)
        parts.append(jnp.dot(placing, block[:rows, :], preferred_element_type=F32))
    packed[...] = jnp.concatenate(parts, axis=0).astype(BF)
    token[...] = jnp.zeros_like(token)


def pack(at, blocks, following, pieces, rows, choices, cap, after):
    n = len(blocks)
    shapes = [((n * cap, blocks[0].shape[1]), BF), ((n, blocks[0].shape[0] - rows, rows), F32)]
    out = [jax.ShapeDtypeStruct(*a) for a in shapes] + [jax.ShapeDtypeStruct(a.shape, BF) for a in following]
    kernel = functools.partial(pack_kernel, choices, len(following), len(pieces))
    operands = (at, *blocks, *following, *pieces)
    specs = [SMEM] + [None] * (len(operands) - 1)
    packed, labels, *rest, token = call(kernel, out + side_by_side(pieces), specs, operands, after, PACK)
    return packed, labels, rest[:len(following)], rest[len(following):], token


def pair_kernel(keep, rec, *refs):
    *outs, token = refs
    feats = outs[0].shape[1]
    for s, out in enumerate(outs):
        here = slice(s * feats, (s + 1) * feats)
        out[...] = (keep[:, here].astype(F32) + rec[:, here].astype(F32)).astype(out.dtype)
    token[...] = jnp.zeros_like(token)


def pair_sum(keep, rec, feats, after):
    rows, width = keep.shape
    out = [jax.ShapeDtypeStruct((rows, feats), BF if s else F32) for s in range(width // feats)]
    *outs, token = call(pair_kernel, out, [None] * 2, (keep, rec), after, PAIR)
    return outs, token


def spread_kernel(choices, at, labels, *refs):
    *terms, stay, go, token = refs
    total = terms[0][...].astype(F32)
    for a in terms[1:]:
        total = total + a[...].astype(F32)
    cap = total.shape[0] // 2
    across = (((0,), (0,)), ((), ()))
    for u, out in enumerate((stay, go)):
        here = total[u * cap:(u + 1) * cap].astype(BF)
        placing, weight = placing_of(labels[u], at[0], cap, choices)
        table = jnp.where(placing, weight, 0.0)
        high = table.astype(BF)
        low = (table - high.astype(F32)).astype(BF)
        value = lax.dot_general(high, here, across, preferred_element_type=F32)
        value += lax.dot_general(low, here, across, preferred_element_type=F32)
        out[...] = value.astype(out.dtype)
    token[...] = jnp.zeros_like(token)


def spread(at, labels, choices, terms, after):
    shape = (labels.shape[2], terms[0].shape[1])
    out = [jax.ShapeDtypeStruct(shape, F32), jax.ShapeDtypeStruct(shape, BF)]
    kernel = functools.partial(spread_kernel, choices)
    return call(kernel, out, [SMEM] + [None] * (1 + len(terms)), (at, labels, *terms), after, SPREAD)


def expert_kernel(half, order, near, far, w_gate, w_up, w_down, give, keep, token, gate, up, hidden):
    k = pl.program_id(0)
    both = 2 * half

    def first(rows):
        gate[...] += jnp.dot(rows[...], w_gate[...], preferred_element_type=F32)
        up[...] += jnp.dot(rows[...], w_up[...], preferred_element_type=F32)

    @pl.when(k == 0)
    def _():
        gate[...] = jnp.zeros_like(gate)
        up[...] = jnp.zeros_like(up)
        token[...] = jnp.zeros_like(token)

    pl.when(k < half)(functools.partial(first, near))
    pl.when((k >= half) & (k < both))(functools.partial(first, far))

    @pl.when(k == both - 1)
    def _():
        v = gate[...]
        hidden[...] = (v / (1.0 + jnp.exp(-v)) * up[...]).astype(BF)

    def second(out):
        out[...] = jnp.dot(hidden[...], w_down[...], preferred_element_type=F32).astype(BF)

    pl.when((k >= both) & (k < both + half))(functools.partial(second, give))
    pl.when(k >= both + half)(functools.partial(second, keep))


def expert(order, near, far, feats, w_gate, w_up, w_down, after):
    rows, width = near.shape
    units = w_gate.shape[2]
    half = width // feats
    both = 2 * half
    into = pl.BlockSpec((None, feats, units), lambda k, order: (0, order[jnp.minimum(k, both - 1)], 0))

    def part(first):
        return pl.BlockSpec((rows, feats), lambda k, order: (0, jnp.clip(k - first, 0, half - 1)))

    grid = pltpu.PrefetchScalarGridSpec(
        num_scalar_prefetch=1,
        grid=(2 * both,),
        in_specs=[part(0), part(half), into, into]
        + [pl.BlockSpec((None, units, feats), lambda k, order: (0, 0, order[jnp.maximum(k, both)]))]
        + [pl.BlockSpec(memory_space=pl.ANY)] * len(after),
        out_specs=[part(both), part(both + half), pl.BlockSpec((8, 128), lambda k, order: (0, 0))],
        scratch_shapes=[pltpu.VMEM((rows, units), F32)] * 2 + [pltpu.VMEM((rows, units), BF)],
    )
    return pl.pallas_call(
        behind(functools.partial(expert_kernel, half), 6, len(after)),
        grid_spec=grid,
        out_shape=[jax.ShapeDtypeStruct((rows, width), BF)] * 2 + [TOKEN],
        compiler_params=pltpu.CompilerParams(vmem_limit_bytes=EXPERT_MIB * 2**20),
        cost_estimate=hint(EXPERT),
    )(order, near, far, w_gate, w_up, w_down, *after)


def local(tokens, routes, gate_weights, w_gate, w_up, w_down):
    groups, inners = lax.axis_size("group"), lax.axis_size("inner")
    g, i = lax.axis_index("group"), lax.axis_index("inner")
    chips, planes = inners // 2, groups // 2
    x, c = i // 2, i % 2
    rows, feats = tokens.shape
    cap = rows * routes.shape[1] * 3 // (2 * groups)

    def over_y(a):
        return lax.ppermute(a, "group", [(j, j ^ 1) for j in range(groups)])

    def over_z(a):
        return lax.ppermute(a, "group", [(j, (j + 2) % groups) for j in range(groups)])

    def over_core(a):
        return lax.ppermute(a, "inner", [(j, j ^ 1) for j in range(inners)])

    def over_x(a, s):
        return lax.ppermute(a, "inner", [(j, (j + 2 * s) % inners) for j in range(inners)])

    came = [(x - s) % chips * 2 for s in range(chips)]
    goes = [(x + s) % chips * 2 for s in range(chips)]
    order = jnp.stack(
        [k + c for k in came] + [k + 1 - c for k in came] + [k + 1 - c for k in goes] + [k + c for k in goes]
    ).astype(jnp.int32)

    at = jnp.full((1,), g, jnp.int32)
    block, token = label(tokens, routes, gate_weights, [])
    main, other = [block] + [over_z(block)] * (planes > 1), [over_y(block)]
    choices = routes.shape[1]

    labels, pieces, near, kept, given, own, passed, back, total = {}, {}, {}, {}, {}, {}, {}, {}, None
    stay = {}
    for step, t in schedule(planes):
        if step == "pack":
            after = [token] + ([given[t - 3]] if t - 3 in given else [])
            blocks, before = (main[t], other[t]), pieces.get(t - 1, [])
            p, labels[t], ahead, whole, token = pack(at, blocks, main[t + 1:], before, rows, choices, cap, after)
            other += [over_y(a) for a in ahead]
            main += [over_z(a) for a in ahead if t + 2 < planes]
            pieces[t] = [p] + [over_x(p, s) for s in range(1, chips)]
            near.update((t - 1, (a, over_core(a))) for a in whole)
        elif step == "join":
            a, token = join(pieces[t], [token])
            near[t] = a, over_core(a)
        elif step == "expert":
            give, kept[t], token = expert(order, *near[t], feats, w_gate, w_up, w_down, [token])
            given[t] = over_core(give)
        elif step == "pair":
            (own[t], *sums), token = pair_sum(kept[t], given[t], feats, [token])
            passed[t] = [over_x(a, s + 1) for s, a in enumerate(sums)]
        else:
            stay[t], go, token = spread(at, labels[t], choices, [own[t], *passed[t]], [token])
            back[t] = over_y(go)
            value = stay[t] + back[t].astype(F32)
            total = (value if total is None else value + over_z(total).astype(F32)).astype(BF)
    return total


def schedule(planes):
    last = planes - 1
    steps = [("pack", 0)]
    for t in range(1, planes):
        steps += [("pack", t), ("expert", t - 1)]
    steps += [("join", last), ("expert", last)]
    steps += [("pair", t) for t in range(last - 1, 0, -1)]
    for t in range(1, planes):
        if t == max(last - 1, 1):
            steps += [("pair", last)]
        steps += [("spread", t)]
    return steps + [("pair", 0), ("spread", 0)]


def solution(mesh):
    placed = (
        P("group", "inner"),
        P("group", None),
        P("group", None),
        P("group", None, "inner"),
        P("group", None, "inner"),
        P("group", "inner", None),
    )
    return jax.shard_map(
        local, mesh=mesh, in_specs=placed, out_specs=P("group", "inner"), check_vma=False
    )
```

```python
import functools

import jax
import jax.numpy as jnp
from jax import lax
from jax.experimental import pallas as pl
from jax.experimental.pallas import tpu as pltpu
from jax.sharding import PartitionSpec as P

BF = jnp.bfloat16
F32 = jnp.float32
TOKEN = jax.ShapeDtypeStruct((8, 128), F32)
PACK, EXPERT, PAIR, SPREAD, LABEL = 10, 40, 2, 20, 1
VMEM_MIB, EXPERT_MIB = 12, 22


def behind(kernel, reads, after):
    return lambda *refs: kernel(*refs[:reads], *refs[reads + after:])


def call(kernel, out_shape, specs, operands, after, us, mib=VMEM_MIB):
    vmem = pl.BlockSpec(memory_space=pltpu.VMEM)
    return pl.pallas_call(
        behind(kernel, len(operands), len(after)),
        in_specs=[s or vmem for s in specs] + [pl.BlockSpec(memory_space=pl.ANY)] * len(after),
        out_specs=[vmem] * (len(out_shape) + 1),
        out_shape=[*out_shape, TOKEN],
        compiler_params=pltpu.CompilerParams(vmem_limit_bytes=mib * 2**20),
        cost_estimate=hint(us),
    )(*operands, *after)


def hint(us):
    return pl.CostEstimate(flops=int(us * 1e9), bytes_accessed=1024, transcendentals=0)


SMEM = pl.BlockSpec(memory_space=pltpu.SMEM)


def label_kernel(tokens, routes, weights, block, token):
    rows = tokens.shape[0]
    block[:rows, :] = tokens[...]
    w = weights[...]
    high = w.astype(BF).astype(F32)
    middle = (w - high).astype(BF).astype(F32)
    low = w - high - middle
    spare = block.shape[0] - rows - 4 * w.shape[0]
    parts = [routes[...].astype(F32), high, middle, low] + [jnp.zeros((spare, rows), F32)] * (spare > 0)
    block[rows:, :rows] = jnp.concatenate(parts, axis=0).astype(BF)
    if block.shape[1] > rows:
        block[rows:, rows:] = jnp.zeros((block.shape[0] - rows, block.shape[1] - rows), BF)
    token[...] = jnp.zeros_like(token)


def label(tokens, routes, gate_weights, after):
    rows, feats = tokens.shape
    extra = -(-4 * routes.shape[1] // 16) * 16
    out = [jax.ShapeDtypeStruct((rows + extra, feats), BF)]
    return call(label_kernel, out, [None] * 3, (tokens, routes.T, gate_weights.T), after, LABEL)


def placing_of(labels, me, cap, choices):
    rows = labels.shape[1]
    named = labels[:choices] == me.astype(F32)
    weights = labels[choices:2 * choices] + labels[2 * choices:3 * choices] + labels[3 * choices:4 * choices]
    weight = jnp.sum(jnp.where(named, weights, 0.0), axis=0, keepdims=True)
    picked = jnp.sum(jnp.where(named, 1.0, 0.0), axis=0, keepdims=True)
    one, two = (lax.broadcasted_iota(jnp.int32, (rows, rows), n) for n in (0, 1))
    before = jnp.where(one < two, 1.0, 0.0).astype(BF)
    many = jnp.broadcast_to(picked, (16, rows)).astype(BF)
    slot = jnp.dot(many, before, preferred_element_type=F32)[:1]
    slot = jnp.where(picked > 0.5, slot, -1.0).astype(jnp.int32)
    return lax.broadcasted_iota(jnp.int32, (cap, rows), 0) == slot, weight


def joined(pieces, near):
    feats = pieces[0].shape[1]
    for n, piece in enumerate(pieces):
        near[:, n * feats:(n + 1) * feats] = piece[...]


def join_kernel(*refs):
    *pieces, near, token = refs
    joined(pieces, near)
    token[...] = jnp.zeros_like(token)


def side_by_side(pieces):
    return [jax.ShapeDtypeStruct((pieces[0].shape[0], len(pieces) * pieces[0].shape[1]), BF)] if pieces else []


def join(pieces, after):
    return call(join_kernel, side_by_side(pieces), [None] * len(pieces), pieces, after, PACK)


def pack_kernel(choices, ahead, before, at, *refs):
    blocks, following, pieces = refs[:2], refs[2:2 + ahead], refs[2 + ahead:2 + ahead + before]
    packed, labels, *rest, token = refs[2 + ahead + before:]
    for a, b in zip(following, rest[:ahead], strict=True):
        b[...] = a[...]
    if before:
        joined(pieces, rest[ahead])
    rows, cap = labels.shape[2], packed.shape[0] // len(blocks)
    parts = []
    for u, block in enumerate(blocks):
        lines = block[rows:, :rows].astype(F32)
        labels[u] = lines
        placing, _ = placing_of(lines, at[0], cap, choices)
        placing = jnp.where(placing, 1.0, 0.0).astype(BF)
        parts.append(jnp.dot(placing, block[:rows, :], preferred_element_type=F32))
    packed[...] = jnp.concatenate(parts, axis=0).astype(BF)
    token[...] = jnp.zeros_like(token)


def pack(at, blocks, following, pieces, rows, choices, cap, after):
    n = len(blocks)
    shapes = [((n * cap, blocks[0].shape[1]), BF), ((n, blocks[0].shape[0] - rows, rows), F32)]
    out = [jax.ShapeDtypeStruct(*a) for a in shapes] + [jax.ShapeDtypeStruct(a.shape, BF) for a in following]
    kernel = functools.partial(pack_kernel, choices, len(following), len(pieces))
    operands = (at, *blocks, *following, *pieces)
    specs = [SMEM] + [None] * (len(operands) - 1)
    packed, labels, *rest, token = call(kernel, out + side_by_side(pieces), specs, operands, after, PACK)
    return packed, labels, rest[:len(following)], rest[len(following):], token


def pair_kernel(keep, rec, *refs):
    *outs, token = refs
    feats = outs[0].shape[1]
    for s, out in enumerate(outs):
        here = slice(s * feats, (s + 1) * feats)
        out[...] = (keep[:, here].astype(F32) + rec[:, here].astype(F32)).astype(out.dtype)
    token[...] = jnp.zeros_like(token)


def pair_sum(keep, rec, feats, after):
    rows, width = keep.shape
    out = [jax.ShapeDtypeStruct((rows, feats), BF if s else F32) for s in range(width // feats)]
    *outs, token = call(pair_kernel, out, [None] * 2, (keep, rec), after, PAIR)
    return outs, token


def spread_kernel(choices, at, labels, *refs):
    *terms, stay, go, token = refs
    total = terms[0][...].astype(F32)
    for a in terms[1:]:
        total = total + a[...].astype(F32)
    cap = total.shape[0] // 2
    across = (((0,), (0,)), ((), ()))
    for u, out in enumerate((stay, go)):
        here = total[u * cap:(u + 1) * cap].astype(BF)
        placing, weight = placing_of(labels[u], at[0], cap, choices)
        table = jnp.where(placing, weight, 0.0)
        high = table.astype(BF)
        low = (table - high.astype(F32)).astype(BF)
        value = lax.dot_general(high, here, across, preferred_element_type=F32)
        value += lax.dot_general(low, here, across, preferred_element_type=F32)
        out[...] = value.astype(out.dtype)
    token[...] = jnp.zeros_like(token)


def spread(at, labels, choices, terms, after):
    shape = (labels.shape[2], terms[0].shape[1])
    out = [jax.ShapeDtypeStruct(shape, F32), jax.ShapeDtypeStruct(shape, BF)]
    kernel = functools.partial(spread_kernel, choices)
    return call(kernel, out, [SMEM] + [None] * (1 + len(terms)), (at, labels, *terms), after, SPREAD)


def expert_kernel(half, order, near, far, w_gate, w_up, w_down, give, keep, token, gate, up, hidden):
    k = pl.program_id(0)
    both = 2 * half

    def first(rows):
        gate[...] += jnp.dot(rows[...], w_gate[...], preferred_element_type=F32)
        up[...] += jnp.dot(rows[...], w_up[...], preferred_element_type=F32)

    @pl.when(k == 0)
    def _():
        gate[...] = jnp.zeros_like(gate)
        up[...] = jnp.zeros_like(up)
        token[...] = jnp.zeros_like(token)

    pl.when(k < half)(functools.partial(first, near))
    pl.when((k >= half) & (k < both))(functools.partial(first, far))

    @pl.when(k == both - 1)
    def _():
        v = gate[...]
        hidden[...] = (v / (1.0 + jnp.exp(-v)) * up[...]).astype(BF)

    def second(out):
        out[...] = jnp.dot(hidden[...], w_down[...], preferred_element_type=F32).astype(BF)

    pl.when((k >= both) & (k < both + half))(functools.partial(second, give))
    pl.when(k >= both + half)(functools.partial(second, keep))


def expert(order, near, far, feats, w_gate, w_up, w_down, after):
    rows, width = near.shape
    units = w_gate.shape[2]
    half = width // feats
    both = 2 * half
    into = pl.BlockSpec((None, feats, units), lambda k, order: (0, order[jnp.minimum(k, both - 1)], 0))

    def part(first):
        return pl.BlockSpec((rows, feats), lambda k, order: (0, jnp.clip(k - first, 0, half - 1)))

    grid = pltpu.PrefetchScalarGridSpec(
        num_scalar_prefetch=1,
        grid=(2 * both,),
        in_specs=[part(0), part(half), into, into]
        + [pl.BlockSpec((None, units, feats), lambda k, order: (0, 0, order[jnp.maximum(k, both)]))]
        + [pl.BlockSpec(memory_space=pl.ANY)] * len(after),
        out_specs=[part(both), part(both + half), pl.BlockSpec((8, 128), lambda k, order: (0, 0))],
        scratch_shapes=[pltpu.VMEM((rows, units), F32)] * 2 + [pltpu.VMEM((rows, units), BF)],
    )
    return pl.pallas_call(
        behind(functools.partial(expert_kernel, half), 6, len(after)),
        grid_spec=grid,
        out_shape=[jax.ShapeDtypeStruct((rows, width), BF)] * 2 + [TOKEN],
        compiler_params=pltpu.CompilerParams(vmem_limit_bytes=EXPERT_MIB * 2**20),
        cost_estimate=hint(EXPERT),
    )(order, near, far, w_gate, w_up, w_down, *after)


def local(tokens, routes, gate_weights, w_gate, w_up, w_down):
    groups, inners = lax.axis_size("group"), lax.axis_size("inner")
    g, i = lax.axis_index("group"), lax.axis_index("inner")
    chips, planes = inners // 2, groups // 2
    x, c = i // 2, i % 2
    rows, feats = tokens.shape
    cap = rows * routes.shape[1] * 3 // (2 * groups)

    def over_y(a):
        return lax.ppermute(a, "group", [(j, j ^ 1) for j in range(groups)])

    def over_z(a):
        return lax.ppermute(a, "group", [(j, (j + 2) % groups) for j in range(groups)])

    def over_core(a):
        return lax.ppermute(a, "inner", [(j, j ^ 1) for j in range(inners)])

    def over_x(a, s):
        return lax.ppermute(a, "inner", [(j, (j + 2 * s) % inners) for j in range(inners)])

    came = [(x - s) % chips * 2 for s in range(chips)]
    goes = [(x + s) % chips * 2 for s in range(chips)]
    order = jnp.stack(
        [k + c for k in came] + [k + 1 - c for k in came] + [k + 1 - c for k in goes] + [k + c for k in goes]
    ).astype(jnp.int32)

    at = jnp.full((1,), g, jnp.int32)
    block, token = label(tokens, routes, gate_weights, [])
    main, other = [block] + [over_z(block)] * (planes > 1), [over_y(block)]
    choices = routes.shape[1]

    labels, pieces, near, kept, given, own, passed, back, total = {}, {}, {}, {}, {}, {}, {}, {}, None
    stay = {}
    for step, t in schedule(planes):
        if step == "pack":
            after = [token] + ([given[t - 3]] if t - 3 in given else [])
            blocks, before = (main[t], other[t]), pieces.get(t - 1, [])
            p, labels[t], ahead, whole, token = pack(at, blocks, main[t + 1:], before, rows, choices, cap, after)
            other += [over_y(a) for a in ahead]
            main += [over_z(a) for a in ahead if t + 2 < planes]
            pieces[t] = [p] + [over_x(p, s) for s in range(1, chips)]
            near.update((t - 1, (a, over_core(a))) for a in whole)
        elif step == "join":
            a, token = join(pieces[t], [token])
            near[t] = a, over_core(a)
        elif step == "expert":
            give, kept[t], token = expert(order, *near[t], feats, w_gate, w_up, w_down, [token])
            given[t] = over_core(give)
        elif step == "pair":
            (own[t], *sums), token = pair_sum(kept[t], given[t], feats, [token])
            passed[t] = [over_x(a, s + 1) for s, a in enumerate(sums)]
        else:
            stay[t], go, token = spread(at, labels[t], choices, [own[t], *passed[t]], [token])
            back[t] = over_y(go)
            value = stay[t] + back[t].astype(F32)
            total = (value if total is None else value + over_z(total).astype(F32)).astype(BF)
    return total


def schedule(planes):
    last = planes - 1
    steps = [("pack", 0)]
    for t in range(1, planes):
        steps += [("pack", t), ("expert", t - 1)] + [("pair", t - 2)] * (t > 2)
    steps += [("join", last)] + [("pair", last - 1)] * (last > 1) + [("expert", last)]
    for t in range(1, planes):
        steps += [("pair", last)] * (t == min(2, last)) + [("spread", t)]
    return steps + [("pair", 0), ("spread", 0)]


def solution(mesh):
    placed = (
        P("group", "inner"),
        P("group", None),
        P("group", None),
        P("group", None, "inner"),
        P("group", None, "inner"),
        P("group", "inner", None),
    )
    return jax.shard_map(
        local, mesh=mesh, in_specs=placed, out_specs=P("group", "inner"), check_vma=False
    )
```

```python
import functools

import jax
import jax.numpy as jnp
from jax import lax
from jax.experimental import pallas as pl
from jax.experimental.pallas import tpu as pltpu
from jax.sharding import PartitionSpec as P

BF = jnp.bfloat16
F32 = jnp.float32
TOKEN = jax.ShapeDtypeStruct((8, 128), F32)
PACK, EXPERT, PAIR, SPREAD, LABEL = 10, 40, 2, 40, 1
VMEM_MIB, STREAM_MIB, LAST_MIB = 12, 50, 36


def behind(kernel, reads, after):
    return lambda *refs: kernel(*refs[:reads], *refs[reads + after:])


def call(kernel, out_shape, specs, operands, after, us, mib=VMEM_MIB):
    vmem = pl.BlockSpec(memory_space=pltpu.VMEM)
    return pl.pallas_call(
        behind(kernel, len(operands), len(after)),
        in_specs=[s or vmem for s in specs] + [pl.BlockSpec(memory_space=pl.ANY)] * len(after),
        out_specs=[vmem] * (len(out_shape) + 1),
        out_shape=[*out_shape, TOKEN],
        compiler_params=pltpu.CompilerParams(vmem_limit_bytes=mib * 2**20),
        cost_estimate=hint(us),
    )(*operands, *after)


def hint(us):
    return pl.CostEstimate(flops=int(us * 1e9), bytes_accessed=1024, transcendentals=0)


SMEM = pl.BlockSpec(memory_space=pltpu.SMEM)


def label_kernel(tokens, routes, weights, block, token):
    rows = tokens.shape[0]
    block[:rows, :] = tokens[...]
    w = weights[...]
    high = w.astype(BF).astype(F32)
    middle = (w - high).astype(BF).astype(F32)
    low = w - high - middle
    spare = block.shape[0] - rows - 4 * w.shape[0]
    parts = [routes[...].astype(F32), high, middle, low] + [jnp.zeros((spare, rows), F32)] * (spare > 0)
    block[rows:, :rows] = jnp.concatenate(parts, axis=0).astype(BF)
    if block.shape[1] > rows:
        block[rows:, rows:] = jnp.zeros((block.shape[0] - rows, block.shape[1] - rows), BF)
    token[...] = jnp.zeros_like(token)


def label(tokens, routes, gate_weights, after):
    rows, feats = tokens.shape
    extra = -(-4 * routes.shape[1] // 16) * 16
    out = [jax.ShapeDtypeStruct((rows + extra, feats), BF)]
    return call(label_kernel, out, [None] * 3, (tokens, routes.T, gate_weights.T), after, LABEL)


def placing_of(labels, me, cap, choices):
    rows = labels.shape[1]
    named = labels[:choices] == me.astype(F32)
    weights = labels[choices:2 * choices] + labels[2 * choices:3 * choices] + labels[3 * choices:4 * choices]
    weight = jnp.sum(jnp.where(named, weights, 0.0), axis=0, keepdims=True)
    picked = jnp.sum(jnp.where(named, 1.0, 0.0), axis=0, keepdims=True)
    one, two = (lax.broadcasted_iota(jnp.int32, (rows, rows), n) for n in (0, 1))
    before = jnp.where(one < two, 1.0, 0.0).astype(BF)
    many = jnp.broadcast_to(picked, (16, rows)).astype(BF)
    slot = jnp.dot(many, before, preferred_element_type=F32)[:1]
    slot = jnp.where(picked > 0.5, slot, -1.0).astype(jnp.int32)
    return lax.broadcasted_iota(jnp.int32, (cap, rows), 0) == slot, weight


def joined(pieces, near):
    feats = pieces[0].shape[1]
    for n, piece in enumerate(pieces):
        near[:, n * feats:(n + 1) * feats] = piece[...]


def join_kernel(*refs):
    *pieces, near, token = refs
    joined(pieces, near)
    token[...] = jnp.zeros_like(token)


def side_by_side(pieces):
    return [jax.ShapeDtypeStruct((pieces[0].shape[0], len(pieces) * pieces[0].shape[1]), BF)] if pieces else []


def join(pieces, after):
    return call(join_kernel, side_by_side(pieces), [None] * len(pieces), pieces, after, PACK)


def pack_kernel(choices, ahead, before, at, *refs):
    blocks, following, pieces = refs[:2], refs[2:2 + ahead], refs[2 + ahead:2 + ahead + before]
    packed, labels, *rest, token = refs[2 + ahead + before:]
    for a, b in zip(following, rest[:ahead], strict=True):
        b[...] = a[...]
    if before:
        joined(pieces, rest[ahead])
    rows, cap = labels.shape[2], packed.shape[0] // len(blocks)
    parts = []
    for u, block in enumerate(blocks):
        lines = block[rows:, :rows].astype(F32)
        labels[u] = lines
        placing, _ = placing_of(lines, at[0], cap, choices)
        placing = jnp.where(placing, 1.0, 0.0).astype(BF)
        parts.append(jnp.dot(placing, block[:rows, :], preferred_element_type=F32))
    packed[...] = jnp.concatenate(parts, axis=0).astype(BF)
    token[...] = jnp.zeros_like(token)


def pack(at, blocks, following, pieces, rows, choices, cap, after):
    n = len(blocks)
    shapes = [((n * cap, blocks[0].shape[1]), BF), ((n, blocks[0].shape[0] - rows, rows), F32)]
    out = [jax.ShapeDtypeStruct(*a) for a in shapes] + [jax.ShapeDtypeStruct(a.shape, BF) for a in following]
    kernel = functools.partial(pack_kernel, choices, len(following), len(pieces))
    operands = (at, *blocks, *following, *pieces)
    specs = [SMEM] + [None] * (len(operands) - 1)
    packed, labels, *rest, token = call(kernel, out + side_by_side(pieces), specs, operands, after, PACK)
    return packed, labels, rest[:len(following)], rest[len(following):], token


def pair_kernel(keep, rec, *refs):
    *outs, token = refs
    feats = outs[0].shape[1]
    for s, out in enumerate(outs):
        here = slice(s * feats, (s + 1) * feats)
        out[...] = (keep[:, here].astype(F32) + rec[:, here].astype(F32)).astype(out.dtype)
    token[...] = jnp.zeros_like(token)


def pair_sum(keep, rec, feats, after):
    rows, width = keep.shape
    out = [jax.ShapeDtypeStruct((rows, feats), BF if s else F32) for s in range(width // feats)]
    *outs, token = call(pair_kernel, out, [None] * 2, (keep, rec), after, PAIR)
    return outs, token


def spread_kernel(choices, at, labels, *refs):
    *terms, stay, go, token = refs
    total = terms[0][...].astype(F32)
    for a in terms[1:]:
        total = total + a[...].astype(F32)
    cap = total.shape[0] // 2
    across = (((0,), (0,)), ((), ()))
    for u, out in enumerate((stay, go)):
        here = total[u * cap:(u + 1) * cap].astype(BF)
        placing, weight = placing_of(labels[u], at[0], cap, choices)
        table = jnp.where(placing, weight, 0.0)
        high = table.astype(BF)
        low = (table - high.astype(F32)).astype(BF)
        value = lax.dot_general(high, here, across, preferred_element_type=F32)
        value += lax.dot_general(low, here, across, preferred_element_type=F32)
        out[...] = value.astype(out.dtype)
    token[...] = jnp.zeros_like(token)


def spread(at, labels, choices, terms, after):
    shape = (labels.shape[2], terms[0].shape[1])
    out = [jax.ShapeDtypeStruct(shape, F32), jax.ShapeDtypeStruct(shape, BF)]
    kernel = functools.partial(spread_kernel, choices)
    return call(kernel, out, [SMEM] + [None] * (1 + len(terms)), (at, labels, *terms), after, SPREAD)


def expert_kernel(half, order, near, far, w_gate, w_up, w_down, give, keep, token, gate, up, hidden):
    k = pl.program_id(0)
    both = 2 * half

    def first(rows):
        gate[...] += jnp.dot(rows[...], w_gate[...], preferred_element_type=F32)
        up[...] += jnp.dot(rows[...], w_up[...], preferred_element_type=F32)

    @pl.when(k == 0)
    def _():
        gate[...] = jnp.zeros_like(gate)
        up[...] = jnp.zeros_like(up)
        token[...] = jnp.zeros_like(token)

    pl.when(k < half)(functools.partial(first, near))
    pl.when((k >= half) & (k < both))(functools.partial(first, far))

    @pl.when(k == both - 1)
    def _():
        v = gate[...]
        hidden[...] = (v / (1.0 + jnp.exp(-v)) * up[...]).astype(BF)

    def second(out):
        out[...] = jnp.dot(hidden[...], w_down[...], preferred_element_type=F32).astype(BF)

    pl.when((k >= both) & (k < both + half))(functools.partial(second, give))
    pl.when(k >= both + half)(functools.partial(second, keep))


def expert(order, near, far, feats, w_gate, w_up, w_down, after, mib):
    rows, width = near.shape
    units = w_gate.shape[2]
    half = width // feats
    both = 2 * half
    into = pl.BlockSpec((None, feats, units), lambda k, order: (0, order[jnp.minimum(k, both - 1)], 0))

    def part(first):
        return pl.BlockSpec((rows, feats), lambda k, order: (0, jnp.clip(k - first, 0, half - 1)))

    grid = pltpu.PrefetchScalarGridSpec(
        num_scalar_prefetch=1,
        grid=(2 * both,),
        in_specs=[part(0), part(half), into, into]
        + [pl.BlockSpec((None, units, feats), lambda k, order: (0, 0, order[jnp.maximum(k, both)]))]
        + [pl.BlockSpec(memory_space=pl.ANY)] * len(after),
        out_specs=[part(both), part(both + half), pl.BlockSpec((8, 128), lambda k, order: (0, 0))],
        scratch_shapes=[pltpu.VMEM((rows, units), F32)] * 2 + [pltpu.VMEM((rows, units), BF)],
    )
    return pl.pallas_call(
        behind(functools.partial(expert_kernel, half), 6, len(after)),
        grid_spec=grid,
        out_shape=[jax.ShapeDtypeStruct((rows, width), BF)] * 2 + [TOKEN],
        compiler_params=pltpu.CompilerParams(vmem_limit_bytes=mib * 2**20),
        cost_estimate=hint(EXPERT),
    )(order, near, far, w_gate, w_up, w_down, *after)


def local(tokens, routes, gate_weights, w_gate, w_up, w_down):
    groups, inners = lax.axis_size("group"), lax.axis_size("inner")
    g, i = lax.axis_index("group"), lax.axis_index("inner")
    chips, planes = inners // 2, groups // 2
    x, c = i // 2, i % 2
    rows, feats = tokens.shape
    cap = rows * routes.shape[1] * 3 // (2 * groups)

    def over_y(a):
        return lax.ppermute(a, "group", [(j, j ^ 1) for j in range(groups)])

    def over_z(a):
        return lax.ppermute(a, "group", [(j, (j + 2) % groups) for j in range(groups)])

    def over_core(a):
        return lax.ppermute(a, "inner", [(j, j ^ 1) for j in range(inners)])

    def over_x(a, s):
        return lax.ppermute(a, "inner", [(j, (j + 2 * s) % inners) for j in range(inners)])

    came = [(x - s) % chips * 2 for s in range(chips)]
    goes = [(x + s) % chips * 2 for s in range(chips)]
    order = jnp.stack(
        [k + c for k in came] + [k + 1 - c for k in came] + [k + 1 - c for k in goes] + [k + c for k in goes]
    ).astype(jnp.int32)

    at = jnp.full((1,), g, jnp.int32)
    block, token = label(tokens, routes, gate_weights, [])
    main, other = [block] + [over_z(block)] * (planes > 1), [over_y(block)]
    choices = routes.shape[1]

    labels, pieces, near, kept, given, own, passed, back, total = {}, {}, {}, {}, {}, {}, {}, {}, None
    stay = {}
    for step, t in schedule(planes):
        if step == "pack":
            after = [token] + ([given[t - 3]] if t - 3 in given else [])
            blocks, before = (main[t], other[t]), pieces.get(t - 1, [])
            p, labels[t], ahead, whole, token = pack(at, blocks, main[t + 1:], before, rows, choices, cap, after)
            other += [over_y(a) for a in ahead]
            main += [over_z(a) for a in ahead if t + 2 < planes]
            pieces[t] = [p] + [over_x(p, s) for s in range(1, chips)]
            near.update((t - 1, (a, over_core(a))) for a in whole)
        elif step == "join":
            a, token = join(pieces[t], [token])
            near[t] = a, over_core(a)
        elif step == "expert":
            give, kept[t], token = expert(order, *near[t], feats, w_gate, w_up, w_down, [token], STREAM_MIB if t < planes - 1 else LAST_MIB)
            given[t] = over_core(give)
        elif step == "pair":
            (own[t], *sums), token = pair_sum(kept[t], given[t], feats, [token])
            passed[t] = [over_x(a, s + 1) for s, a in enumerate(sums)]
        else:
            stay[t], go, token = spread(at, labels[t], choices, [own[t], *passed[t]], [token])
            back[t] = over_y(go)
            value = stay[t] + back[t].astype(F32)
            total = (value if total is None else value + over_z(total).astype(F32)).astype(BF)
    return total


def schedule(planes):
    last = planes - 1
    steps = [("pack", 0)]
    for t in range(1, planes):
        steps += [("pack", t), ("expert", t - 1)] + [("pair", t - 2)] * (t > 2)
    steps += [("join", last)] + [("pair", last - 1)] * (last > 1) + [("expert", last)]
    for t in range(1, planes):
        steps += [("pair", last)] * (t == min(2, last)) + [("spread", t)]
    return steps + [("pair", 0), ("spread", 0)]


def solution(mesh):
    placed = (
        P("group", "inner"),
        P("group", None),
        P("group", None),
        P("group", None, "inner"),
        P("group", None, "inner"),
        P("group", "inner", None),
    )
    return jax.shard_map(
        local, mesh=mesh, in_specs=placed, out_specs=P("group", "inner"), check_vma=False
    )
```
